256 devices in a mesh: outer: 8 (over z_lo, x), inner: 32 (over z_hi, y, core).
Axes of the slice: x: 4, y: 4, z: 8 (z_hi: 4, z_lo: 2; z = z_hi * 2 + z_lo), core: 2. Of those that a mesh axis runs over, the one named last changes fastest.
Arguments:
- queries: bfloat16 [32768, 2048], P(('outer', 'inner')), may hold values from -8 to 8
- keys: bfloat16 [32768, 512], P(('outer', 'inner')), may hold values from -8 to 8
- values: bfloat16 [32768, 512], P(('outer', 'inner')), may hold values from -6 to 6
- teacher: bfloat16 [32768, 2048], P(('outer', 'inner')), may hold values from -6 to 6
- flags: int32 [256, 256], P(('outer', 'inner')), may hold values from 0 to 1, as said below
- slots: int32 [256], replicated, may hold values from 0 to 255, each once
Outputs:
- grad_queries: float32 [32768, 2048], P(('outer', 'inner'))
- grad_keys: float32 [32768, 512], P(('outer', 'inner'))
- grad_values: float32 [32768, 512], P(('outer', 'inner'))
The draws below stay inside these ranges and needn't reach their ends.
Inputs may be any that keep to these rules, and one draw needn't show every extreme that they name: With shards numbered s = o * 32 + i, flags[a, b] can be 1 only if b's shard has the outer index o of a's shard and an inner index i - k (cyclically) with 0 <= k < 12, or has inner index i and another outer index. `slots`: each slot once.
All inputs are finite; a program needn't handle non-finite values.
Results may differ from the reference program's by a relative error of at most 0.015.
Values may be sent and summed in bfloat16 or wider, within the bound.
A program may use at most 128 MiB of HBM per device.

```python
import jax
import jax.numpy as jnp
from jax import lax

H = 16
KVH = 4
HD = 128
GRP = 4
BLK = 128
TOK_DEV = 128
REACH = 12
NSH = 256
TOKENS = 32768
BPS = 1
NB = 256
NK = 20
N_OUTER = 8
N_INNER = 32


def draw_queries(key, part):
    key = jax.random.fold_in(key, 1)
    base_key = jax.random.fold_in(key, 0)
    out = jnp.clip(jax.random.normal(base_key, (TOKENS, H * HD), jnp.float32), -8.0, 8.0)
    return out.astype(jnp.bfloat16)


def draw_keys(key, part):
    key = jax.random.fold_in(key, 2)
    out = jnp.clip(jax.random.normal(key, (TOKENS, KVH * HD), jnp.float32), -8.0, 8.0)
    return out.astype(jnp.bfloat16)


def draw_flags(key, part):
    key = jax.random.fold_in(key, 3)
    level_key, bit_key = jax.random.split(key)
    blocks = jnp.arange(NB, dtype=jnp.int32)
    shard = blocks // BPS
    outer_of = shard // N_INNER
    inner_of = shard % N_INNER
    same_outer = outer_of[:, None] == outer_of[None, :]
    back = (inner_of[:, None] - inner_of[None, :]) % N_INNER
    support = same_outer & (back < REACH) | (inner_of[:, None] == inner_of[None, :]) & jnp.logical_not(same_outer)
    level = jax.random.randint(level_key, (NSH,), 1, 8)
    bits = jax.random.randint(bit_key, (NB, NB), 0, 8)
    return jnp.where(support & (bits < level[shard][:, None]), 1, 0).astype(jnp.int32)


def block_levels(key, extent, pieces, smallest, high):
    def one(axis_at, shards_of):
        draws = jax.random.uniform(jax.random.fold_in(jax.random.fold_in(key, 6), axis_at), (shards_of,), jnp.float32, smallest / len(pieces), high / len(pieces))
        return jnp.repeat(jnp.exp(draws), extent[axis_at] // shards_of).reshape((-1,) + (1,) * (len(extent) - axis_at - 1))

    level = one(*pieces[0])
    for cut in pieces[1:]:
        level = level * one(*cut)
    return level


def scatter_about(rng, dims, width, most, cuts=(), held_as=jnp.bfloat16):
    drawn = width * jax.random.normal(rng, dims, jnp.float32)
    if cuts:
        drawn = drawn * block_levels(rng, dims, cuts, -0.22, 0.18)
    return jnp.clip(drawn, -most, most).astype(held_as)


def setup_inputs(seed: int = 0) -> dict:
    streams_of = jax.random.split(jax.random.key(seed), 7)
    return {
        "queries": draw_queries(jax.random.fold_in(streams_of[6], 71), 0),
        "keys": draw_keys(jax.random.fold_in(streams_of[6], 71), 0),
        "values": scatter_about(streams_of[2], (TOKENS, KVH * HD), 1.0, 6.0, ((0, 256),)),
        "teacher": scatter_about(streams_of[3], (TOKENS, H * HD), 1.0, 6.0, ((0, 256),)),
        "flags": draw_flags(jax.random.fold_in(streams_of[6], 71), 0),
        "slots": jax.random.permutation(streams_of[5], NSH).astype(jnp.int32),
    }


NEG = -1.0e30


def visible_keys(flag_rows, slots, me, ids, valid, rows, block):
    local = jnp.arange(rows, dtype=jnp.int32)
    per_shard = flag_rows.shape[0]
    count = ids.shape[0]
    cols = (ids[:, None] * per_shard + (local // block)[None, :]).reshape(-1).astype(jnp.int32)
    looked = jnp.repeat(jnp.take(flag_rows, cols, axis=1), block, axis=0).reshape(rows, count, rows)
    q_pos = slots[me] * rows + local
    k_pos = slots[ids][:, None] * rows + local[None, :]
    same = (ids == me)[None, :, None] & ((local // block)[:, None, None] == (local // block)[None, None, :])
    permitted_tiles = valid[None, :, None] & ((looked != 0) | same) & (k_pos[None, :, :] <= q_pos[:, None, None])
    return permitted_tiles.reshape(rows, count * rows)


def key_shards(shard):
    outer_idx = shard // N_INNER
    inner_idx = shard % N_INNER
    back = jnp.arange(REACH, dtype=jnp.int32)
    inner_ids = outer_idx * N_INNER + (inner_idx - back) % N_INNER
    groups = jnp.arange(N_OUTER, dtype=jnp.int32)
    outer_ids = groups * N_INNER + inner_idx
    ids = jnp.concatenate([inner_ids, outer_ids]).astype(jnp.int32)
    valid = jnp.concatenate([jnp.ones((REACH,), bool), groups != outer_idx])
    return ids, valid


def reference(queries, keys, values, teacher, flags, slots):
    scale = 1.0 / (HD ** 0.5)
    q_sh = queries.reshape(NSH, TOK_DEV, H * HD)
    k_sh = keys.reshape(NSH, TOK_DEV, KVH * HD)
    v_sh = values.reshape(NSH, TOK_DEV, KVH * HD)
    t_sh = teacher.reshape(NSH, TOK_DEV, H * HD)

    def one(carry, shard):
        dk_tot, dv_tot = carry
        ids, valid = key_shards(shard)
        flag_rows = lax.dynamic_slice_in_dim(flags, shard * BPS, BPS, 0)
        permitted_tiles = visible_keys(flag_rows, slots, shard, ids, valid, TOK_DEV, BLK)[:, None, None, :]
        qh = q_sh[shard].reshape(TOK_DEV, KVH, GRP, HD).astype(jnp.float32)
        kk = k_sh[ids].reshape(NK * TOK_DEV, KVH, HD).astype(jnp.float32)
        vv = v_sh[ids].reshape(NK * TOK_DEV, KVH, HD).astype(jnp.float32)
        scores = jnp.einsum('tkgd,skd->tkgs', qh, kk) * scale
        top = jnp.max(jnp.where(permitted_tiles, scores, NEG), axis=-1)
        weights = jnp.where(permitted_tiles, jnp.exp(scores - top[..., None]), 0.0)
        total = jnp.sum(weights, axis=-1)
        weights_b = lax.optimization_barrier(weights.astype(jnp.bfloat16)).astype(jnp.float32)
        attended = jnp.einsum('tkgs,skd->tkgd', weights_b, vv) / total[..., None]
        target = t_sh[shard].reshape(TOK_DEV, KVH, GRP, HD).astype(jnp.float32)
        resid = attended - target
        dout = lax.optimization_barrier(resid.astype(jnp.bfloat16)).astype(jnp.float32)
        delta = jnp.sum(resid * attended, axis=-1)
        lse = top + jnp.log(total)
        prob = jnp.where(permitted_tiles, jnp.exp(scores - lse[..., None]), 0.0)
        prob_b = lax.optimization_barrier(prob.astype(jnp.bfloat16)).astype(jnp.float32)
        grad_v = jnp.einsum('tkgs,tkgd->skd', prob_b, dout)
        dprob = jnp.einsum('tkgd,skd->tkgs', dout, vv)
        dscore = prob * (dprob - delta[..., None])
        dscore_b = lax.optimization_barrier(dscore.astype(jnp.bfloat16)).astype(jnp.float32)
        grad_q = jnp.einsum('tkgs,skd->tkgd', dscore_b, kk) * scale
        grad_k = jnp.einsum('tkgs,tkgd->skd', dscore_b, qh) * scale
        dk_tot = dk_tot.at[ids].add(grad_k.reshape(NK, TOK_DEV, KVH * HD))
        dv_tot = dv_tot.at[ids].add(grad_v.reshape(NK, TOK_DEV, KVH * HD))
        return (dk_tot, dv_tot), grad_q.reshape(TOK_DEV, H * HD)

    start = jnp.zeros((NSH, TOK_DEV, KVH * HD), jnp.float32)
    (dk_all, dv_all), dq_all = lax.scan(one, (start, start), jnp.arange(NSH, dtype=jnp.int32))
    return (dq_all.reshape(TOKENS, H * HD), dk_all.reshape(TOKENS, KVH * HD), dv_all.reshape(TOKENS, KVH * HD))
```

```python
import jax
import jax.numpy as jnp
from jax import lax
from jax.experimental import pallas as pl
from jax.experimental.pallas import tpu as pltpu
from jax.sharding import PartitionSpec as P

H = 16
KVH = 4
HD = 128
GRP = 4
TOK = 128
ROW = GRP * TOK

NC = 2
CPH = KVH // NC
CW = CPH * HD

SCALE = 1.0 / HD**0.5
LOG2E = 1.4426950408889634
C1 = SCALE * LOG2E
BIG = 1.0e30

OWN = 0
X1, X3, ZZ, P4, X2, Q4, ZX1, ZX3, P1, P3, Q1, Q3, P2, P5, Q2, Q5, ZX2, E = range(1, 19)
NS = 19
PAIRS = 9

f32, bf16 = jnp.float32, jnp.bfloat16
MESH = pl.DeviceIdType.MESH


def dot(a, b, lhs_dim=1):
    return lax.dot_general(a, b, (((lhs_dim,), (0,)), ((), ())), preferred_element_type=f32)


def kernel(
    q_hbm, k_hbm, v_hbm, t_hbm, flags, slots,
    dq_ref, dk_ref, dv_ref,
    kv, g, r, own, qraw, traw, qt, qs, tt, do_n, do_t, delta,
    wb, mb, mrun, tot, acc, dqt, bias,
    lsem, gs_sem, gr_sem, rs_sem, rr_sem,
):
    o, i = lax.axis_index("outer"), lax.axis_index("inner")
    zl, x = o // 4, o % 4
    u, c = i // 2, i % 2
    y = u % 4

    def at(zl_, x_, u_, c_):
        return (zl_ * 4 + (x_ + 4) % 4, ((u_ + 16) % 16) * 2 + c_)

    def along_y(d):
        return at(zl, x, (u // 4) * 4 + (y + d + 4) % 4, c)

    sib = at(zl, x, u, 1 - c)
    xp, xm = at(zl, x + 1, u, c), at(zl, x - 1, u, c)
    zo = at(1 - zl, x, u, c)
    zp, zm = at(zl, x, u + 4, c), at(zl, x, u - 4, c)
    yp, ym, y2 = along_y(1), along_y(-1), along_y(2)
    up, um = at(zl, x, u + 1, c), at(zl, x, u - 1, c)
    e_to = at(zl, x, u + 2 * c, 1 - c)
    e_back = at(zl, x, u - 2 * (1 - c), 1 - c)
    skew = at(zl, x, u - 2 + 4 * c, 1 - c)

    barrier = pltpu.get_barrier_semaphore()
    partners = (sib, xp, xm, zo, zp, zm, yp, ym, y2, up, um, skew)
    for d in partners:
        pl.semaphore_signal(barrier, inc=1, device_id=d, device_id_type=MESH)

    def load(src, dst, n):
        return pltpu.make_async_copy(src, dst, lsem.at[n])

    loads = []
    for h in range(NC):
        cols = pl.ds(h * CW, CW)
        loads.append(load(k_hbm.at[:, cols], kv.at[OWN, h, 0], 2 * h))
        loads.append(load(v_hbm.at[:, cols], kv.at[OWN, h, 1], 2 * h + 1))
    loads.append(load(q_hbm, qraw, 2 * NC))
    loads.append(load(t_hbm, traw, 2 * NC + 1))
    for cp in loads:
        cp.start()

    me = o * 32 + i
    mine = slots[me]

    def note(slot, shard):
        seen = (flags[0, shard] == 1) & (slots[shard] <= mine)
        bias[slot] = jnp.where(seen, 0.0, BIG).astype(f32)

    def inner_id(back):
        return o * 32 + (i - back + 32) % 32

    for k, (p_slot, q_slot) in enumerate(((P1, Q1), (P2, Q2), (P3, Q3), (P4, Q4), (P5, Q5)), 1):
        note(p_slot, inner_id(2 * k))
        note(q_slot, inner_id(2 * k - 1 + 2 * c))
    note(E, inner_id(11 - 10 * c))
    for slot, dz, dx in ((X1, 0, 3), (X2, 0, 2), (X3, 0, 1), (ZZ, 1, 0), (ZX1, 1, 3), (ZX2, 1, 2), (ZX3, 1, 1)):
        note(slot, (((zl + dz) % 2) * 4 + (x + dx) % 4) * 32 + i)

    def part(ref, slot, h, kvi):
        return ref.at[slot, h] if kvi is None else ref.at[slot, h, kvi]

    def copy(src, dst, s_sems, r_sems, src_slot, slot, h, to, kvi):
        n = 0 if kvi is None else kvi
        return pltpu.make_async_remote_copy(
            src_ref=part(src, src_slot, h, kvi),
            dst_ref=part(dst, slot, h, kvi),
            send_sem=s_sems.at[slot, h, n],
            recv_sem=r_sems.at[slot, h, n],
            device_id=to,
            device_id_type=MESH,
        )

    def gat(src_slot, slot, h, to, kvi=None):
        return copy(kv, kv, gs_sem, gr_sem, src_slot, slot, h, to, kvi)

    def ret(slot, h, to, kvi=None):
        return copy(g, r, rs_sem, rr_sem, slot, slot, h, to, kvi)

    def got(slot, h, kvi=None):
        gat(slot, slot, h, sib, kvi).wait_recv()

    def back(slot, h, kvi=None):
        ret(slot, h, sib, kvi).wait_recv()

    SPLIT = (X1, X3, X2, ZX1, ZX3, ZX2)

    def first_sends(h):
        gat(OWN, P4, h, zp).start()
        gat(OWN, ZZ, h, zo).start()
        for kvi in (0, 1):
            gat(OWN, X1, h, xp, kvi).start()
            gat(OWN, X3, h, xm, 1 - kvi).start()

        @pl.when(y < 3)
        def _():
            gat(OWN, P1, h, yp).start()

        @pl.when(y < 2)
        def _():
            gat(OWN, P2, h, y2).start()

        @pl.when(y == 0)
        def _():
            gat(OWN, P3, h, ym).start()

        @pl.when(c == 0)
        def _():
            gat(OWN, E, h, e_to).start()

    def f0(h):
        got(P4, h)
        gat(P4, Q4, h, sib).start()

        @pl.when(y == 3)
        def _():
            gat(P4, P1, h, yp).start()

        @pl.when(y >= 1)
        def _():
            gat(P4, P3, h, ym).start()

        gat(P4, P5, h, up).start()

        @pl.when(y >= 2)
        def _():
            gat(P4, P2, h, y2).start()

        @pl.when(c == 1)
        def _():
            gat(P4, E, h, e_to).start()

    def f1(h):
        got(ZZ, h)
        for kvi in (0, 1):
            gat(ZZ, ZX1, h, xp, kvi).start()
            gat(ZZ, ZX3, h, xm, 1 - kvi).start()

    def f2(h):
        got(X1, h, 0)
        gat(X1, X2, h, xp, 0).start()
        got(X3, h, 1)
        gat(X3, X2, h, xm, 1).start()

    def f3(h):
        got(P1, h)
        gat(P1, Q1, h, sib).start()
        got(P3, h)
        gat(P3, Q3, h, sib).start()

    def f4(h):
        got(P2, h)
        gat(P2, Q2, h, sib).start()
        got(P5, h)
        gat(P5, Q5, h, sib).start()

    def f5(h):
        got(ZX1, h, 0)
        gat(ZX1, ZX2, h, xp, 0).start()
        got(ZX3, h, 1)
        gat(ZX3, ZX2, h, xm, 1).start()

    def need(j, h):
        if j == 0:
            got(X1, h, 1)
            got(X3, h, 0)
        elif j == 2:
            got(X2, h, 0)
            got(X2, h, 1)
            got(Q4, h)
        elif j == 3:
            got(ZX1, h, 1)
            got(ZX3, h, 0)
        elif j == 5:
            got(Q1, h)
            got(Q3, h)
        elif j == 7:
            got(Q2, h)
            got(Q5, h)
        elif j == 8:
            got(ZX2, h, 0)
            got(ZX2, h, 1)
            got(E, h)

    def add_into(slot, h, *terms, kvi=None):
        parts = (0, 1) if kvi is None else (kvi,)
        for n in parts:
            total = g[slot, h, n].astype(f32)
            for term in terms:
                total = total + r[term, h, n].astype(f32)
            g[slot, h, n] = total.astype(bf16)

    def b_send_zx2(h):
        ret(ZX2, h, xm, 0).start()
        ret(ZX2, h, xp, 1).start()
        ret(E, h, e_back).start()

    def b_send_q(h, a, b):
        ret(a, h, sib).start()
        ret(b, h, sib).start()

    def b_p25(h):
        back(Q2, h)
        add_into(P2, h, Q2)
        ret(P2, h, y2).start()
        back(Q5, h)
        add_into(P5, h, Q5)
        ret(P5, h, um).start()

    def b_p13(h):
        back(Q1, h)
        add_into(P1, h, Q1)
        ret(P1, h, ym).start()
        back(Q3, h)
        add_into(P3, h, Q3)
        ret(P3, h, yp).start()

    def b_x(h, one, two, three):
        back(two, h, 0)
        add_into(one, h, two, kvi=0)
        ret(one, h, xm, 0).start()
        ret(three, h, xp, 0).start()
        back(two, h, 1)
        add_into(three, h, two, kvi=1)
        ret(three, h, xp, 1).start()
        ret(one, h, xm, 1).start()

    def b_zz(h):
        for slot in (ZX1, ZX3):
            for kvi in (0, 1):
                back(slot, h, kvi)
        add_into(ZZ, h, ZX1, ZX3)
        ret(ZZ, h, zo).start()

    def only(cond, value):
        return jnp.where(cond, value, 0.0)

    def r1(h):
        for slot in (P1, P2, P3, P5, Q4, E):
            back(slot, h)
        for n in (0, 1):
            v1, v2, v3, ve = (r[s, h, n].astype(f32) for s in (P1, P2, P3, E))
            total = g[P4, h, n].astype(f32) + r[Q4, h, n].astype(f32) + r[P5, h, n].astype(f32)
            total += only(y == 3, v1) + only(y >= 2, v2) + only(y >= 1, v3) + only(c == 1, ve)
            g[P4, h, n] = total.astype(bf16)
            own[h, n] += only(y < 3, v1) + only(y < 2, v2) + only(y == 0, v3) + only(c == 0, ve)
        ret(P4, h, zm).start()

    def r2(h):
        for slot in (X1, X3):
            for kvi in (0, 1):
                back(slot, h, kvi)
        back(ZZ, h)
        back(P4, h)
        cols = pl.ds(pl.multiple_of(h * CW, CW), CW)
        for n, out in ((0, dk_ref), (1, dv_ref)):
            total = own[h, n]
            for slot in (X1, X3, ZZ, P4):
                total = total + r[slot, h, n].astype(f32)
            out[:, cols] = total

    keep = lax.broadcasted_iota(jnp.int32, (TOK, ROW), 0) <= (
        lax.broadcasted_iota(jnp.int32, (TOK, ROW), 1) % TOK
    )

    def own_forward(h):
        for cc in range(CPH):
            hc = h * CPH + cc
            k = kv[OWN, h, 0, :, cc * HD : (cc + 1) * HD]
            v = kv[OWN, h, 1, :, cc * HD : (cc + 1) * HD]
            s = jnp.where(keep, dot(k, qt[hc]) * C1, -BIG)
            top = jnp.max(s, axis=0, keepdims=True)
            w = jnp.exp2(s - top)
            tot[cc] = jnp.sum(w, axis=0, keepdims=True)
            w = w.astype(bf16)
            wb[OWN, cc] = w
            mrun[cc] = top
            mb[PAIRS, cc] = top
            acc[cc] = dot(v, w, 0)

    def pair_forward(j, h):
        s0 = 2 * j + 1
        ba, bb = bias[s0], bias[s0 + 1]
        for cc in range(CPH):
            hc = h * CPH + cc
            k = kv[pl.ds(s0, 2), h, 0, :, cc * HD : (cc + 1) * HD].reshape(2 * TOK, HD)
            v = kv[pl.ds(s0, 2), h, 1, :, cc * HD : (cc + 1) * HD].reshape(2 * TOK, HD)
            s = dot(k, qt[hc])
            sa, sb = s[:TOK], s[TOK:]
            before = mrun[cc]
            ta = jnp.max(sa, axis=0, keepdims=True) * C1 - ba
            tb = jnp.max(sb, axis=0, keepdims=True) * C1 - bb
            top = jnp.maximum(before, jnp.maximum(ta, tb))
            shrink = jnp.exp2(before - top)
            wa = jnp.exp2(sa * C1 - (top + ba))
            wbb = jnp.exp2(sb * C1 - (top + bb))
            tot[cc] = tot[cc] * shrink + jnp.sum(wa + wbb, axis=0, keepdims=True)
            w = jnp.concatenate([wa.astype(bf16), wbb.astype(bf16)], axis=0)
            wb[pl.ds(s0, 2), cc] = w.reshape(2, TOK, ROW)
            mrun[cc] = top
            mb[j, cc] = top
            acc[cc] = acc[cc] * shrink + dot(v, w, 0)

    def middle(h):
        for cc in range(CPH):
            hc = h * CPH + cc
            attended = acc[cc] / tot[cc]
            resid = attended - tt[hc].astype(f32)
            dout = resid.astype(bf16)
            do_t[cc] = dout
            do_n[cc] = dout.T
            delta[cc] = jnp.sum(resid * attended, axis=0, keepdims=True)

    def grads(h, hc, cc, j, w, k, v):
        share = jnp.exp2(mb[j, cc] - mrun[cc]) / tot[cc]
        prob = w.astype(f32) * share
        dprob = dot(v, do_t[cc])
        ds = (prob * (dprob - delta[cc])).astype(bf16)
        gv = dot(prob.astype(bf16), do_n[cc])
        gk = dot(ds, qs[hc]) * SCALE
        return gk, gv, dot(k, ds, 0)

    def own_backward(h):
        for cc in range(CPH):
            hc = h * CPH + cc
            k = kv[OWN, h, 0, :, cc * HD : (cc + 1) * HD]
            v = kv[OWN, h, 1, :, cc * HD : (cc + 1) * HD]
            gk, gv, gq = grads(h, hc, cc, PAIRS, wb[OWN, cc], k, v)
            own[h, 0, :, cc * HD : (cc + 1) * HD] = gk
            own[h, 1, :, cc * HD : (cc + 1) * HD] = gv
            dqt[cc] += gq

    def pair_backward(j, h):
        s0 = 2 * j + 1
        for cc in range(CPH):
            hc = h * CPH + cc
            k = kv[pl.ds(s0, 2), h, 0, :, cc * HD : (cc + 1) * HD].reshape(2 * TOK, HD)
            v = kv[pl.ds(s0, 2), h, 1, :, cc * HD : (cc + 1) * HD].reshape(2 * TOK, HD)
            w = wb[pl.ds(s0, 2), cc].reshape(2 * TOK, ROW)
            gk, gv, gq = grads(h, hc, cc, j, w, k, v)
            g[pl.ds(s0, 2), h, 0, :, cc * HD : (cc + 1) * HD] = gk.astype(bf16).reshape(2, TOK, HD)
            g[pl.ds(s0, 2), h, 1, :, cc * HD : (cc + 1) * HD] = gv.astype(bf16).reshape(2, TOK, HD)
            dqt[cc] += gq

    def finish_queries(h):
        for cc in range(CPH):
            for n in range(GRP):
                cols = pl.ds(pl.multiple_of((h * CPH + cc) * ROW + n * HD, HD), HD)
                dq_ref[:, cols] = dqt[cc, :, n * TOK : (n + 1) * TOK].T * SCALE

    pl.semaphore_wait(barrier, len(partners))
    loads[0].wait()
    loads[1].wait()
    first_sends(0)
    for cp in loads[2:]:
        cp.wait()
    for hc in range(KVH):
        for n in range(GRP):
            cols = slice((hc * GRP + n) * HD, (hc * GRP + n + 1) * HD)
            rows = slice(n * TOK, (n + 1) * TOK)
            block = qraw[:, cols]
            qs[hc, rows, :] = block
            qt[hc, :, rows] = block.T
            tt[hc, :, rows] = traw[:, cols].T

    def run(cond, fn, *args):
        @pl.when(cond)
        def _():
            fn(*args)

    def chunk(h, carry):
        first, last = h == 0, h == NC - 1
        own_forward(h)

        def forward(j, carry):
            def when(k, fn, *args):
                run(first & (j == k), fn, *args)

            when(0, f2, h)
            when(1, f0, h)
            when(1, f1, h)
            when(3, f5, h)
            when(4, f3, h)
            when(6, f4, h)
            run((j == 2) & jnp.logical_not(last), first_sends, h + 1)
            run((j == 2) & jnp.logical_not(first), r1, h - 1)
            for k in range(PAIRS):
                if k in (0, 2, 3, 5, 7, 8):
                    run(j == k, need, k, h)
            pair_forward(j, h)
            return carry

        lax.fori_loop(0, PAIRS, forward, 0)
        middle(h)
        dqt[...] = jnp.zeros_like(dqt)

        def backward(j, carry):
            def when(k, fn, *args):
                run(jnp.logical_not(last) & (j == k), fn, *args)

            pair_backward(PAIRS - 1 - j, h)
            run(j == 0, b_send_zx2, h)
            run(j == 1, b_send_q, h, Q2, Q5)
            run(j == 3, b_send_q, h, Q1, Q3)
            run(j == 3, b_p25, h)
            run(j == 5, b_p13, h)
            run(j == 5, b_x, h, ZX1, ZX2, ZX3)
            run(j == 6, ret(X2, h, xm, 0).start)
            run(j == 6, ret(X2, h, xp, 1).start)
            run(j == 6, ret(Q4, h, sib).start)
            when(0, f0, h + 1)
            when(1, f1, h + 1)
            when(2, f2, h + 1)
            when(4, f3, h + 1)
            when(6, f4, h + 1)
            when(7, f5, h + 1)
            run((j == 4) & jnp.logical_not(first), r2, h - 1)
            return carry

        lax.fori_loop(0, PAIRS, backward, 0)
        b_zz(h)
        b_x(h, X1, X2, X3)
        own_backward(h)
        finish_queries(h)
        return carry

    lax.fori_loop(0, NC, chunk, 0)
    r1(NC - 1)
    r2(NC - 1)

    def drain(h, carry):
        for slot in range(1, NS):
            for kvi in (0, 1) if slot in SPLIT else (None,):
                gat(OWN, slot, h, sib, kvi).wait_send()
                ret(slot, h, sib, kvi).wait_send()
        return carry

    lax.fori_loop(0, NC, drain, 0)


def body(queries, keys, values, teacher, flags, slots):
    vmem = pltpu.VMEM
    dma = pltpu.SemaphoreType.DMA
    hbm = pl.BlockSpec(memory_space=pl.ANY)
    smem = pl.BlockSpec(memory_space=pltpu.SMEM)
    out = pl.BlockSpec(memory_space=pltpu.VMEM)
    return pl.pallas_call(
        kernel,
        out_shape=(
            jax.ShapeDtypeStruct((TOK, H * HD), f32),
            jax.ShapeDtypeStruct((TOK, KVH * HD), f32),
            jax.ShapeDtypeStruct((TOK, KVH * HD), f32),
        ),
        in_specs=[hbm, hbm, hbm, hbm, smem, smem],
        out_specs=(out, out, out),
        scratch_shapes=[
            vmem((NS, NC, 2, TOK, CW), bf16),
            vmem((NS, NC, 2, TOK, CW), bf16),
            vmem((NS, NC, 2, TOK, CW), bf16),
            vmem((NC, 2, TOK, CW), f32),
            vmem((TOK, H * HD), bf16),
            vmem((TOK, H * HD), bf16),
            vmem((KVH, HD, ROW), bf16),
            vmem((KVH, ROW, HD), bf16),
            vmem((KVH, HD, ROW), bf16),
            vmem((CPH, ROW, HD), bf16),
            vmem((CPH, HD, ROW), bf16),
            vmem((CPH, 1, ROW), f32),
            vmem((NS, CPH, TOK, ROW), bf16),
            vmem((PAIRS + 1, CPH, 1, ROW), f32),
            vmem((CPH, 1, ROW), f32),
            vmem((CPH, 1, ROW), f32),
            vmem((CPH, HD, ROW), f32),
            vmem((CPH, HD, ROW), f32),
            pltpu.SMEM((NS,), f32),
            dma((2 * NC + 2,)),
            dma((NS, NC, 2)),
            dma((NS, NC, 2)),
            dma((NS, NC, 2)),
            dma((NS, NC, 2)),
        ],
        compiler_params=pltpu.CompilerParams(
            collective_id=0, has_side_effects=True, vmem_limit_bytes=56 * 2**20
        ),
        cost_estimate=pl.CostEstimate(flops=9 * 10**9, bytes_accessed=4 * 10**6, transcendentals=5 * 10**6),
    )(queries, keys, values, teacher, flags, slots)


def solution(mesh):
    rows = P(("outer", "inner"), None)
    return jax.shard_map(
        body,
        mesh=mesh,
        in_specs=(rows, rows, rows, rows, rows, P()),
        out_specs=(rows, rows, rows),
        check_vma=False,
    )
```
